256 devices in a mesh: gx: 8 (over y, x_hi), gy: 32 (over z, x_lo, core).
Axes of the slice: x: 4 (x_hi: 2, x_lo: 2; x = x_hi * 2 + x_lo), y: 4, z: 8, core: 2. Of those that a mesh axis runs over, the one named last changes fastest.
Arguments:
- field: float32 [512, 512, 256], P('gx', 'gy'), may hold values from -6 to 6
- weights: float32 [128, 128, 8, 1024], P('gy', 'gx'), may hold values from -1 to 1
- cotangent: float32 [512, 512, 256], P('gx', 'gy'), may hold values from -6 to 6
Outputs:
- output_field: float32 [512, 512, 256], P('gx', 'gy')
- field_grad: float32 [512, 512, 256], P('gx', 'gy')
- weight_grad: float32 [128, 128, 8, 1024], P('gy', 'gx')
The draws below stay inside these ranges and needn't reach their ends.
All inputs are finite; a program needn't handle non-finite values.
Results may differ from the reference program's by a relative error of at most 0.000098.
Values sent between devices are 32-bit elements; how exact they have to be, the bound alone decides.
A program may use at most 128 MiB of HBM per device.

```python
import math
import jax
import jax.numpy as jnp
from jax import lax

NX = 512
NY = 512
MODES = 64
CHANNELS = 32
ZMODES = 8


def block_levels(rng, dims, cuts, low, largest):
    gain = 1.0
    for dim, parts in cuts:
        heights = jax.random.uniform(jax.random.fold_in(jax.random.fold_in(rng, 6), dim), (parts,), jnp.float32, low / len(cuts), largest / len(cuts))
        gain = gain * jnp.repeat(jnp.exp(heights), dims[dim] // parts).reshape((-1,) + (1,) * (len(dims) - 1 - dim))
    return gain


def bell_draw(rng, shape, deviation, limit, shards=(), kind=jnp.bfloat16):
    entries = deviation * jax.random.normal(rng, shape, jnp.float32)
    if shards:
        entries = entries * block_levels(rng, shape, shards, -0.22, 0.18)
    return jnp.clip(entries, -limit, limit).astype(kind)


def setup_inputs(seed: int = 0) -> dict:
    keys = jax.random.split(jax.random.key(seed), 4)
    return {
        "field": bell_draw(keys[0], (NX, NY, ZMODES * CHANNELS), 1.0, 6.0, ((0, 8), (1, 32)), jnp.float32),
        "weights": bell_draw(keys[1], (2 * MODES, 2 * MODES, ZMODES, CHANNELS * CHANNELS), CHANNELS ** -0.5, 1.0, ((0, 32), (1, 8)), jnp.float32),
        "cotangent": bell_draw(keys[2], (NX, NY, ZMODES * CHANNELS), 1.0, 6.0, ((0, 8), (1, 32)), jnp.float32),
    }


highest = lax.Precision.HIGHEST

def basis_table(length, row_count, first_cell, modes):
    wave_index = lax.iota(jnp.int32, 2 * modes)[:, None]
    positions = first_cell + lax.iota(jnp.int32, row_count)[None, :]
    frequency = jnp.where(wave_index < modes, wave_index, wave_index - modes + 1)
    phase_steps = frequency * positions % length
    angles = 2.0 * math.pi / length * phase_steps.astype(jnp.float32)
    values = jnp.where(wave_index < modes, jnp.cos(angles), jnp.sin(angles))
    return (math.sqrt(2.0 / length) * values).astype(jnp.float32)

def mix_modes(coefs, weights):
    lead_y, lead_x, width = coefs.shape
    zcount = weights.shape[2]
    chans = width // zcount
    split_coefs = coefs.reshape(lead_y, lead_x, zcount, chans)
    split_weights = weights.reshape(lead_y, lead_x, zcount, chans, chans)
    mixed = jnp.einsum('abzi,abzio->abzo', split_coefs, split_weights, precision=highest)
    return mixed.reshape(lead_y, lead_x, width)

def reference(field, weights, cotangent):
    table_x = basis_table(NX, NX, 0, MODES)
    table_y = basis_table(NY, NY, 0, MODES)

    def forward(field_in, weights_in):
        xmodes = jnp.einsum('kx,xyc->kyc', table_x, field_in, precision=highest)
        coefs = jnp.einsum('ly,kyc->lkc', table_y, xmodes, precision=highest)
        mixed = mix_modes(coefs, weights_in)
        back = jnp.einsum('ly,lkc->ykc', table_y, mixed, precision=highest)
        return jnp.einsum('kx,ykc->xyc', table_x, back, precision=highest)
    output_field, pullback = jax.vjp(forward, field, weights)
    field_grad, weight_grad = pullback(cotangent)
    return (output_field, field_grad, weight_grad)
```

```python
import math

import jax
import jax.numpy as jnp
from jax import lax
from jax.sharding import PartitionSpec as P

NX = 512
NY = 512
MODES = 64
CHANNELS = 32


high = lax.Precision.HIGH


def basis_table(length, modes):
    wave_index = lax.iota(jnp.int32, 2 * modes)[:, None]
    positions = lax.iota(jnp.int32, length)[None, :]
    frequency = jnp.where(wave_index < modes, wave_index, wave_index - modes + 1)
    phase_steps = frequency * positions % length
    angles = 2.0 * math.pi / length * phase_steps.astype(jnp.float32)
    values = jnp.where(wave_index < modes, jnp.cos(angles), jnp.sin(angles))
    return math.sqrt(2.0 / length) * values


def project(pair, table_x, table_y):
    cells = lax.all_to_all(pair, "gx", split_axis=3, concat_axis=1, tiled=True)
    xmodes = jnp.einsum("kx,fxyc->fkyc", table_x, cells, precision=high)
    columns = lax.all_to_all(xmodes, "gy", split_axis=1, concat_axis=2, tiled=True)
    modes = jnp.einsum("ly,fkyc->flkc", table_y, columns, precision=high)
    owned = lax.all_to_all(modes, "gy", split_axis=1, concat_axis=2, tiled=True)
    return lax.all_to_all(owned, "gx", split_axis=2, concat_axis=3, tiled=True)


def expand(pair, table_x, table_y):
    owned = lax.all_to_all(pair, "gx", split_axis=3, concat_axis=2, tiled=True)
    modes = lax.all_to_all(owned, "gy", split_axis=2, concat_axis=1, tiled=True)
    columns = jnp.einsum("ly,flkc->fkyc", table_y, modes, precision=high)
    xmodes = lax.all_to_all(columns, "gy", split_axis=2, concat_axis=1, tiled=True)
    cells = jnp.einsum("kx,fkyc->fxyc", table_x, xmodes, precision=high)
    return lax.all_to_all(cells, "gx", split_axis=1, concat_axis=3, tiled=True)


def body(field, weights, cotangent):
    owned_y, owned_x, zcount, square = weights.shape
    width = field.shape[2]
    table_x = basis_table(NX, MODES)
    table_y = basis_table(NY, MODES)
    split_weights = weights.reshape(owned_y, owned_x, zcount, CHANNELS, CHANNELS)
    both = project(jnp.stack([field, cotangent]), table_x, table_y)
    both = both.reshape(2, owned_y, owned_x, zcount, CHANNELS)
    coefs, grads = both[0], both[1]
    mixed = jnp.einsum("abzi,abzio->abzo", coefs, split_weights, precision=lax.Precision.HIGHEST)
    dmixed = jnp.einsum("abzio,abzo->abzi", split_weights, grads, precision=lax.Precision.HIGHEST)
    weight_grad = coefs[..., :, None] * grads[..., None, :]
    back = jnp.stack([mixed, dmixed]).reshape(2, owned_y, owned_x, width)
    out = expand(back, table_x, table_y)
    return out[0], out[1], weight_grad.reshape(weights.shape)


def solution(mesh):
    in_specs = (P("gx", "gy", None), P("gy", "gx", None, None), P("gx", "gy", None))
    out_specs = (P("gx", "gy", None), P("gx", "gy", None), P("gy", "gx", None, None))
    return jax.shard_map(body, mesh=mesh, in_specs=in_specs, out_specs=out_specs, check_vma=False)
```

```python
import math

import jax
import jax.numpy as jnp
import numpy as np
from jax import lax
from jax.experimental import pallas as pl
from jax.experimental.pallas import tpu as pltpu
from jax.sharding import PartitionSpec as P

N = 512
MODES = 64
GX = 8
GY = 32
F32 = jnp.float32
BF16 = jnp.bfloat16
MESH = pl.DeviceIdType.MESH


def basis_table():
    k = np.arange(2 * MODES)[:, None]
    p = np.arange(N)[None, :]
    frequency = np.where(k < MODES, k, k - MODES + 1)
    angles = 2.0 * math.pi / N * ((frequency * p) % N)
    values = math.sqrt(2.0 / N) * np.where(k < MODES, np.cos(angles), np.sin(angles))
    return values.reshape(32, 4, N).transpose(1, 0, 2).reshape(128, N)


def split_table(values):
    values = values.astype(np.float32)
    high = values.astype(BF16)
    low = (values - high.astype(np.float32)).astype(BF16)
    return high, low


def halves(value):
    high = value.astype(BF16)
    return high, (value - high.astype(F32)).astype(BF16)


def dot(a, b):
    return jnp.dot(a, b, preferred_element_type=F32)


def swap_blocks(v):
    lane = lax.broadcasted_iota(jnp.int32, v[0].shape, 1)
    low = lane < 64
    even = (lane // 32) % 2 == 0
    a0 = jnp.where(low, v[0], pltpu.roll(v[2], 64, 1))
    a1 = jnp.where(low, v[1], pltpu.roll(v[3], 64, 1))
    a2 = jnp.where(low, pltpu.roll(v[0], 64, 1), v[2])
    a3 = jnp.where(low, pltpu.roll(v[1], 64, 1), v[3])
    return [
        jnp.where(even, a0, pltpu.roll(a1, 32, 1)),
        jnp.where(even, pltpu.roll(a0, 96, 1), a1),
        jnp.where(even, a2, pltpu.roll(a3, 32, 1)),
        jnp.where(even, pltpu.roll(a2, 96, 1), a3),
    ]


def kernel(
    field, cotangent, weights, table_in, table_out,
    output_field, field_grad, weight_grad,
    cells, w, fwd, inv, spread, expanded, wgrad, result,
    sa, ra, sb, rb, sc, rc, sd, rd, se, re, sf, rf,
    in_sem, out_sem, a_send, a_recv, b_send, b_recv, c_send, c_recv,
    d_send, d_recv, e_send, e_recv, f_send, f_recv,
):
    i = lax.axis_index("gx")
    j = lax.axis_index("gy")

    def at(gx, gy):
        return {"gx": gx, "gy": gy}

    loads = [
        pltpu.make_async_copy(src, dst, in_sem.at[n])
        for n, (src, dst) in enumerate(
            [(field, cells.at[0]), (cotangent, cells.at[1]), (table_in, fwd), (weights, w), (table_out, inv)]
        )
    ]
    for load in loads:
        load.start()

    barrier = pltpu.get_barrier_semaphore()

    def greet(gx, gy):
        pl.semaphore_signal(barrier, inc=1, device_id=at(gx, gy), device_id_type=MESH)

    def greet_x(v, carry):
        greet((i + v) % GX, j)
        return carry

    def greet_y(v, carry):
        other = (j + v) % GY
        greet(i, other)
        greet(j // 4, other)
        greet((i + v // 4) % GX, 4 * i + v % 4)
        return carry

    lax.fori_loop(0, GX, greet_x, 0)
    lax.fori_loop(0, GY, greet_y, 0)

    def send(src, dst, send_sem, recv_sem, gx, gy):
        here = jnp.logical_and(gx == i, gy == j)

        @pl.when(jnp.logical_not(here))
        def _():
            pltpu.make_async_remote_copy(
                src_ref=src, dst_ref=dst, send_sem=send_sem, recv_sem=recv_sem,
                device_id=at(gx, gy), device_id_type=MESH,
            ).start()

        @pl.when(here)
        def _():
            pltpu.make_async_copy(src, dst, recv_sem).start()

    def wait(ref, sem):
        pltpu.make_async_copy(ref, ref, sem).wait()

    def pack_cells(n, u):
        for t in range(2):
            for h in range(2):
                v = [cells[n, :, 8 * u + 4 * t + s, pl.ds(128 * h, 128)] for s in range(4)]
                for b, value in enumerate(swap_blocks(v)):
                    sa[n, u, 4 * h + b, :, pl.ds(128 * t, 128)] = value

    def send_cells(n, u):
        def step(v, carry):
            other = (i + v) % GX
            send(sa.at[n, u, other], ra.at[n, u, i], a_send.at[n, u], a_recv.at[n, u], other, j)
            return carry

        lax.fori_loop(0, GX, step, 0)

    def project(data):
        high, low = halves(data)
        first = dot(fwd[...], high)
        return first[:128] + first[128:] + dot(fwd[:128], low)

    def expand(data):
        high, low = halves(data)
        return dot(inv[...], jnp.concatenate([high, high, low], axis=0))

    def project_x(n, u):
        wait(ra.at[n, u], a_recv.at[n, u])
        modes = project(ra[n, u].reshape(N, 256))
        for t in range(2):
            v = [modes[32 * r : 32 * r + 32, 128 * t : 128 * t + 128] for r in range(4)]
            for s, value in enumerate(swap_blocks(v)):
                sb[n, :, 8 * u + 4 * t + s, :] = value

    def send_columns(n, src, dst, send_sem, recv_sem):
        def step(v, carry):
            other = (j + v) % GY
            send(src.at[n, other], dst.at[n, j], send_sem.at[n], recv_sem.at[n], i, other)
            return carry

        lax.fori_loop(0, GY, step, 0)

    def project_y(n):
        wait(rb.at[n], b_recv.at[n])
        modes = project(rb[n].reshape(N, 128))
        for a in range(4):
            sc[n, :, a, :] = modes[32 * a : 32 * a + 32]

        def step(v, carry):
            other = (j + v) % GY
            send(sc.at[n, other], rc.at[n, i, j % 4], c_send.at[n], c_recv.at[n], j // 4, other)
            return carry

        lax.fori_loop(0, GY, step, 0)

    def owned_modes(n):
        wait(rc.at[n], c_recv.at[n])
        return jnp.concatenate([rc[n, :, q, a, :] for a in range(4) for q in range(4)], axis=0)

    def send_mixed(n, value):
        for a in range(4):
            for q in range(4):
                row = 8 * (4 * a + q)
                sd[n, :, q, a, :] = value[row : row + 8]

        def step(v, carry):
            z = (i + v // 4) % GX
            q = v % 4
            send(sd.at[n, z, q], rd.at[n, j], d_send.at[n], d_recv.at[n], z, 4 * i + q)
            return carry

        lax.fori_loop(0, GY, step, 0)

    def mix():
        high, low = halves(owned_modes(0))
        folded = []
        for r in range(4):
            part = spread[:, pl.ds(1024 * r, 1024)]
            wide = dot(high, part) + dot(low, part)
            expanded[:, pl.ds(1024 * r, 1024)] = wide
            product = wide * w[:, :, r].reshape(128, 1024)
            total = product[:, :128]
            for t in range(1, 8):
                total = total + product[:, 128 * t : 128 * t + 128]
            folded.append(total)
        parts = swap_blocks(folded)
        send_mixed(0, (parts[0] + parts[1]) + (parts[2] + parts[3]))

    def mix_back():
        grads = owned_modes(1)
        tiled = swap_blocks([grads] * 4)
        total = None
        for r in range(4):
            part = spread[:, pl.ds(1024 * r, 1024)]
            product = w[:, :, r].reshape(128, 1024) * jnp.concatenate([tiled[r]] * 8, axis=1)
            high, low = halves(product)
            dims = (((1,), (1,)), ((), ()))
            term = lax.dot_general(high, part, dims, preferred_element_type=F32)
            term = term + lax.dot_general(low, part, dims, preferred_element_type=F32)
            total = term if total is None else total + term
        send_mixed(1, total)
        return tiled

    def outer(tiled):
        for r in range(4):
            value = expanded[:, pl.ds(1024 * r, 1024)] * jnp.concatenate([tiled[r]] * 8, axis=1)
            wgrad[:, :, r] = value.reshape(4, 4, 8, 1024)

    def expand_y(n):
        wait(rd.at[n], d_recv.at[n])
        modes = jnp.concatenate([rd[n, :, a, :] for a in range(4)], axis=0)
        se[n] = expand(modes).reshape(GY, 16, 128)
        send_columns(n, se, re, e_send, e_recv)

    def expand_x(n, u):
        rows = [[] for _ in range(4)]
        for t in range(2):
            v = [re[n, :, 8 * u + 4 * t + s, :] for s in range(4)]
            for r, value in enumerate(swap_blocks(v)):
                rows[r].append(value)
        modes = jnp.concatenate([jnp.concatenate(row, axis=1) for row in rows], axis=0)
        sf[n, u] = expand(modes).reshape(GX, 64, 256)

        def step(v, carry):
            other = (i + v) % GX
            send(sf.at[n, u, other], rf.at[n, u, i], f_send.at[n, u], f_recv.at[n, u], other, j)
            return carry

        lax.fori_loop(0, GX, step, 0)

    def unpack_cells(n, u):
        wait(rf.at[n, u], f_recv.at[n, u])
        for t in range(2):
            for h in range(2):
                v = [rf[n, u, 4 * h + b, :, pl.ds(128 * t, 128)] for b in range(4)]
                for s, value in enumerate(swap_blocks(v)):
                    result[n, :, 8 * u + 4 * t + s, pl.ds(128 * h, 128)] = value

    loads[0].wait()
    pack_cells(0, 0)
    pl.semaphore_wait(barrier, GX + 3 * GY)
    send_cells(0, 0)
    pack_cells(0, 1)
    send_cells(0, 1)
    loads[1].wait()
    for u in range(2):
        pack_cells(1, u)
        send_cells(1, u)

    column = lax.broadcasted_iota(jnp.int32, (128, 4096), 1)
    row = lax.broadcasted_iota(jnp.int32, (128, 4096), 0)
    spread[...] = jnp.where(column // 32 == row, 1.0, 0.0).astype(BF16)

    loads[2].wait()
    for n in range(2):
        for u in range(2):
            project_x(n, u)
        send_columns(n, sb, rb, b_send, b_recv)
    loads[3].wait()
    for n in range(2):
        project_y(n)
    mix()
    tiled = mix_back()
    loads[4].wait()
    for n in range(2):
        expand_y(n)
    for n in range(2):
        wait(re.at[n], e_recv.at[n])
        for u in range(2):
            expand_x(n, u)
    outer(tiled)
    stores = [pltpu.make_async_copy(wgrad, weight_grad, out_sem.at[2])]
    stores[0].start()
    for n, target in enumerate([output_field, field_grad]):
        for u in range(2):
            unpack_cells(n, u)
        store = pltpu.make_async_copy(result.at[n], target, out_sem.at[n])
        store.start()
        stores.append(store)

    for n in range(2):
        for u in range(2):
            wait(sa.at[n, u, pl.ds(0, GX - 1)], a_send.at[n, u])
            wait(sf.at[n, u, pl.ds(0, GX - 1)], f_send.at[n, u])
        wait(sb.at[n, pl.ds(0, GY - 1)], b_send.at[n])
        wait(se.at[n, pl.ds(0, GY - 1)], e_send.at[n])

    inside = i == j // 4

    @pl.when(inside)
    def _():
        for n in range(2):
            wait(sc.at[n, pl.ds(0, GY - 1)], c_send.at[n])
            wait(rd.at[n, pl.ds(0, GY - 1)], d_send.at[n])

    @pl.when(jnp.logical_not(inside))
    def _():
        for n in range(2):
            wait(sc.at[n], c_send.at[n])
            wait(rd.at[n], d_send.at[n])

    for store in stores:
        store.wait()


def body(field, weights, cotangent):
    high, low = split_table(basis_table())
    table_in = jnp.asarray(np.concatenate([high, low], axis=0))
    table_out = jnp.asarray(np.concatenate([high.T, low.T, high.T], axis=1))
    shape = jax.ShapeDtypeStruct
    anywhere = pl.BlockSpec(memory_space=pl.ANY)
    vmem = pltpu.VMEM
    dma = pltpu.SemaphoreType.DMA
    cell_block = vmem((2, 2, GX, 64, 256), F32)
    column_block = vmem((2, GY, 16, 128), F32)
    out = pl.pallas_call(
        kernel,
        out_shape=(
            shape(field.shape, F32),
            shape(field.shape, F32),
            shape((4, 4, 4, 8, 1024), F32),
        ),
        in_specs=[anywhere] * 5,
        out_specs=(anywhere,) * 3,
        scratch_shapes=[
            vmem((2, 64, 16, 256), F32),
            vmem((4, 4, 4, 8, 1024), F32),
            vmem((256, N), BF16),
            vmem((N, 384), BF16),
            vmem((128, 4096), BF16),
            vmem((128, 4096), F32),
            vmem((4, 4, 4, 8, 1024), F32),
            vmem((2, 64, 16, 256), F32),
            cell_block, cell_block,
            column_block, column_block,
            vmem((2, GY, 4, 128), F32), vmem((2, GX, 4, 4, 128), F32),
            vmem((2, GX, 4, 4, 128), F32), vmem((2, GY, 4, 128), F32),
            column_block, column_block,
            cell_block, cell_block,
            dma((5,)), dma((3,)),
            dma((2, 2)), dma((2, 2)),
            dma((2,)), dma((2,)),
            dma((2,)), dma((2,)),
            dma((2,)), dma((2,)),
            dma((2,)), dma((2,)),
            dma((2, 2)), dma((2, 2)),
        ],
        compiler_params=pltpu.CompilerParams(
            collective_id=0, has_side_effects=True, vmem_limit_bytes=56 * 1024 * 1024
        ),
        name="spectral",
    )(field, cotangent, weights.reshape(4, 4, 4, 8, 1024), table_in, table_out)
    return out[0], out[1], out[2].reshape(weights.shape)


def solution(mesh):
    in_specs = (P("gx", "gy", None), P("gy", "gx", None, None), P("gx", "gy", None))
    out_specs = (P("gx", "gy", None), P("gx", "gy", None), P("gy", "gx", None, None))
    return jax.shard_map(body, mesh=mesh, in_specs=in_specs, out_specs=out_specs, check_vma=False)
```

```python
import math

import jax
import jax.numpy as jnp
import numpy as np
from jax import lax
from jax.experimental import pallas as pl
from jax.experimental.pallas import tpu as pltpu
from jax.sharding import PartitionSpec as P

N = 512
MODES = 64
GX = 8
GY = 32
ORDER = (1, 2, 3, 4, 5, 6, 7)
F32 = jnp.float32
BF16 = jnp.bfloat16
MESH = pl.DeviceIdType.MESH


def basis_table():
    k = np.arange(2 * MODES)[:, None]
    p = np.arange(N)[None, :]
    frequency = np.where(k < MODES, k, k - MODES + 1)
    angles = 2.0 * math.pi / N * ((frequency * p) % N)
    values = math.sqrt(2.0 / N) * np.where(k < MODES, np.cos(angles), np.sin(angles))
    return values.reshape(32, 4, N).transpose(1, 0, 2).reshape(128, N)


def split_table(values):
    values = values.astype(np.float32)
    high = values.astype(BF16)
    low = (values - high.astype(np.float32)).astype(BF16)
    return high, low


def halves(value):
    high = value.astype(BF16)
    return high, (value - high.astype(F32)).astype(BF16)


def spread_matrix():
    column = lax.broadcasted_iota(jnp.int32, (128, 4096), 1)
    row = lax.broadcasted_iota(jnp.int32, (128, 4096), 0)
    return jnp.where(column // 32 == row, 1.0, 0.0).astype(BF16)


def dot(a, b):
    return jnp.dot(a, b, preferred_element_type=F32)


def swap_blocks(v):
    lane = lax.broadcasted_iota(jnp.int32, v[0].shape, 1)
    low = lane < 64
    even = (lane // 32) % 2 == 0
    a0 = jnp.where(low, v[0], pltpu.roll(v[2], 64, 1))
    a1 = jnp.where(low, v[1], pltpu.roll(v[3], 64, 1))
    a2 = jnp.where(low, pltpu.roll(v[0], 64, 1), v[2])
    a3 = jnp.where(low, pltpu.roll(v[1], 64, 1), v[3])
    return [
        jnp.where(even, a0, pltpu.roll(a1, 32, 1)),
        jnp.where(even, pltpu.roll(a0, 96, 1), a1),
        jnp.where(even, a2, pltpu.roll(a3, 32, 1)),
        jnp.where(even, pltpu.roll(a2, 96, 1), a3),
    ]


def kernel(
    field, cotangent, weights, table_in, table_out, table_in_y, table_out_y,
    rf, weight_grad,
    cells, w, fwd, inv, fwd_y, inv_y, spread, expanded, wgrad,
    sa, ra, sb, rb, sc, rc, sd, rd, se, re, sf,
    in_sem, out_sem, a_send, a_recv, b_send, b_recv, c_send, c_recv,
    d_send, d_recv, e_send, e_recv, f_send, f_recv,
):
    i = lax.axis_index("gx")
    j = lax.axis_index("gy")

    def at(gx, gy):
        return {"gx": gx, "gy": gy}

    loads = [
        pltpu.make_async_copy(src, dst, in_sem.at[n])
        for n, (src, dst) in enumerate(
            [(field, cells.at[0]), (cotangent, cells.at[1]), (table_in, fwd), (table_in_y, fwd_y), (weights, w), (table_out_y, inv_y), (table_out, inv)]
        )
    ]
    for load in loads:
        load.start()

    barrier = pltpu.get_barrier_semaphore()

    def greet(gx, gy):
        pl.semaphore_signal(barrier, inc=1, device_id=at(gx, gy), device_id_type=MESH)

    def greet_x(v, carry):
        greet((i + v) % GX, j)
        return carry

    def greet_y(v, carry):
        other = (j + v) % GY
        greet(i, other)
        greet(j // 4, other)
        greet((i + v // 4) % GX, 4 * i + v % 4)
        return carry

    lax.fori_loop(0, GX, greet_x, 0)
    lax.fori_loop(0, GY, greet_y, 0)

    def send(src, dst, send_sem, recv_sem, gx, gy):
        here = jnp.logical_and(gx == i, gy == j)

        @pl.when(jnp.logical_not(here))
        def _():
            pltpu.make_async_remote_copy(
                src_ref=src, dst_ref=dst, send_sem=send_sem, recv_sem=recv_sem,
                device_id=at(gx, gy), device_id_type=MESH,
            ).start()

        @pl.when(here)
        def _():
            pltpu.make_async_copy(src, dst, recv_sem).start()

    def wait(ref, sem):
        pltpu.make_async_copy(ref, ref, sem).wait()

    def pack_cells(n, u):
        for t in range(2):
            for h in range(2):
                v = [cells[n, :, 8 * u + 4 * t + s, pl.ds(128 * h, 128)] for s in range(4)]
                for b, value in enumerate(swap_blocks(v)):
                    sa[n, u, 4 * h + b, :, pl.ds(128 * t, 128)] = value

    def send_x(src, dst, send_sem, recv_sem, n, u, part):
        rows = pl.ds(32 * part, 32)
        for v in ORDER:
            other = (i + v) % GX
            pltpu.make_async_remote_copy(
                src_ref=src.at[n, u, other, rows], dst_ref=dst.at[n, u, i, rows],
                send_sem=send_sem.at[n, u], recv_sem=recv_sem.at[n, u],
                device_id=at(other, j), device_id_type=MESH,
            ).start()
        pltpu.make_async_copy(src.at[n, u, i, rows], dst.at[n, u, i, rows], recv_sem.at[n, u]).start()

    def send_cells(n, u, part):
        send_x(sa, ra, a_send, a_recv, n, u, part)

    def send_result(n, u, part):
        send_x(sf, rf, f_send, f_recv, n, u, part)

    def project(table, data):
        high, low = halves(data)
        first = dot(table, high)
        return first[:128] + first[128:] + dot(table[:128], low)

    def expand(table, data):
        high, low = halves(data)
        return dot(table, jnp.concatenate([high, high, low], axis=0))

    def project_x(n, u):
        wait(ra.at[n, u], a_recv.at[n, u])
        modes = project(fwd[...], ra[n, u].reshape(N, 256))
        for t in range(2):
            v = [modes[32 * r : 32 * r + 32, 128 * t : 128 * t + 128] for r in range(4)]
            for s, value in enumerate(swap_blocks(v)):
                sb[n, u, :, 4 * t + s, :] = value
        send_columns(n, u, sb, rb, b_send, b_recv)

    def send_columns(n, u, src, dst, send_sem, recv_sem):
        def step(v, carry):
            other = (j + v) % GY
            send(src.at[n, u, other], dst.at[n, u, j], send_sem.at[n, u], recv_sem.at[n, u], i, other)
            return carry

        lax.fori_loop(0, GY, step, 0)

    def project_y(n):
        parts = []
        for u in range(2):
            wait(rb.at[n, u], b_recv.at[n, u])
            parts.append(project(fwd_y[:, pl.ds(256 * u, 256)], rb[n, u].reshape(256, 128)))
        modes = parts[0] + parts[1]
        for a in range(4):
            sc[n, :, a, :] = modes[32 * a : 32 * a + 32]

        def step(v, carry):
            other = (j + v) % GY
            send(sc.at[n, other], rc.at[n, i, j % 4], c_send.at[n], c_recv.at[n], j // 4, other)
            return carry

        lax.fori_loop(0, GY, step, 0)

    def owned_modes(n):
        wait(rc.at[n], c_recv.at[n])
        return jnp.concatenate([rc[n, :, q, a, :] for a in range(4) for q in range(4)], axis=0)

    def send_mixed(n, value):
        for a in range(4):
            for q in range(4):
                row = 8 * (4 * a + q)
                sd[n, :, q, a, :] = value[row : row + 8]

        def step(v, carry):
            z = (i + v // 4) % GX
            q = v % 4
            send(sd.at[n, z, q], rd.at[n, j], d_send.at[n], d_recv.at[n], z, 4 * i + q)
            return carry

        lax.fori_loop(0, GY, step, 0)

    def mix():
        high, low = halves(owned_modes(0))
        folded = []
        for r in range(4):
            part = spread[:, pl.ds(1024 * r, 1024)]
            wide = dot(high, part) + dot(low, part)
            expanded[:, pl.ds(1024 * r, 1024)] = wide
            product = wide * w[:, :, r].reshape(128, 1024)
            total = product[:, :128]
            for t in range(1, 8):
                total = total + product[:, 128 * t : 128 * t + 128]
            folded.append(total)
        parts = swap_blocks(folded)
        send_mixed(0, (parts[0] + parts[1]) + (parts[2] + parts[3]))

    def mix_back():
        grads = owned_modes(1)
        tiled = swap_blocks([grads] * 4)
        total = None
        for r in range(4):
            part = spread[:, pl.ds(1024 * r, 1024)]
            product = w[:, :, r].reshape(128, 1024) * jnp.concatenate([tiled[r]] * 8, axis=1)
            high, low = halves(product)
            dims = (((1,), (1,)), ((), ()))
            term = lax.dot_general(high, part, dims, preferred_element_type=F32)
            term = term + lax.dot_general(low, part, dims, preferred_element_type=F32)
            total = term if total is None else total + term
        send_mixed(1, total)
        return tiled

    def outer(tiled):
        for r in range(4):
            value = expanded[:, pl.ds(1024 * r, 1024)] * jnp.concatenate([tiled[r]] * 8, axis=1)
            wgrad[:, :, r] = value.reshape(4, 4, 8, 1024)


    def expand_y(n):
        wait(rd.at[n], d_recv.at[n])
        modes = jnp.concatenate([rd[n, :, a, :] for a in range(4)], axis=0)
        for u in range(2):
            rows = expand(inv_y[pl.ds(256 * u, 256), :], modes)
            se[n, u] = rows.reshape(GY, 8, 128)
            send_columns(n, u, se, re, e_send, e_recv)

    def expand_x(n, u):
        wait(re.at[n, u], e_recv.at[n, u])
        rows = [[] for _ in range(4)]
        for t in range(2):
            v = [re[n, u, :, 4 * t + s, :] for s in range(4)]
            for r, value in enumerate(swap_blocks(v)):
                rows[r].append(value)
        modes = jnp.concatenate([jnp.concatenate(row, axis=1) for row in rows], axis=0)
        sf[n, u] = expand(inv[...], modes).reshape(GX, 64, 256)

    loads[0].wait()
    pack_cells(0, 0)
    pack_cells(0, 1)
    pl.semaphore_wait(barrier, GX + 3 * GY)
    for u in range(2):
        for part in range(2):
            send_cells(0, u, part)
    loads[1].wait()
    for u in range(2):
        pack_cells(1, u)
    spread[...] = spread_matrix()
    for load in loads[2:]:
        load.wait()

    project_x(0, 0)
    send_cells(1, 0, 0)
    project_x(0, 1)
    send_cells(1, 0, 1)
    send_cells(1, 1, 0)
    send_cells(1, 1, 1)
    project_y(0)
    project_x(1, 0)
    project_x(1, 1)
    mix()
    project_y(1)
    expand_y(0)
    tiled = mix_back()
    expand_x(0, 0)
    send_result(0, 0, 0)
    send_result(0, 0, 1)
    expand_x(0, 1)
    expand_y(1)
    send_result(0, 1, 0)
    send_result(0, 1, 1)
    outer(tiled)
    store = pltpu.make_async_copy(wgrad, weight_grad, out_sem.at[0])
    store.start()
    for u in range(2):
        expand_x(1, u)
        for part in range(2):
            send_result(1, u, part)

    for n in range(2):
        for u in range(2):
            wait(rf.at[n, u], f_recv.at[n, u])
            wait(sa.at[n, u, pl.ds(0, GX - 1)], a_send.at[n, u])
            wait(sb.at[n, u, pl.ds(0, GY - 1)], b_send.at[n, u])
            wait(se.at[n, u, pl.ds(0, GY - 1)], e_send.at[n, u])
            wait(sf.at[n, u, pl.ds(0, GX - 1)], f_send.at[n, u])

    inside = i == j // 4

    @pl.when(inside)
    def _():
        for n in range(2):
            wait(sc.at[n, pl.ds(0, GY - 1)], c_send.at[n])
            wait(rd.at[n, pl.ds(0, GY - 1)], d_send.at[n])

    @pl.when(jnp.logical_not(inside))
    def _():
        for n in range(2):
            wait(sc.at[n], c_send.at[n])
            wait(rd.at[n], d_send.at[n])

    store.wait()


def finish_kernel(
    received, grad, output_field, field_grad, weight_grad,
    cells, result, passed, load_sem, out_sem, grad_sem, pass_sem,
):
    loads = [
        pltpu.make_async_copy(received.at[n, u], cells.at[n, u], load_sem.at[n, u])
        for n in range(2)
        for u in range(2)
    ]
    passes = [pltpu.make_async_copy(grad.at[a], passed.at[a], grad_sem.at[a]) for a in range(4)]
    for load in loads[:2] + passes + loads[2:]:
        load.start()
    stores = []
    for n, target in enumerate([output_field, field_grad]):
        for u in range(2):
            loads[2 * n + u].wait()
            for t in range(2):
                for h in range(2):
                    v = [cells[n, u, 4 * h + b, :, pl.ds(128 * t, 128)] for b in range(4)]
                    for s, value in enumerate(swap_blocks(v)):
                        result[n, :, 8 * u + 4 * t + s, pl.ds(128 * h, 128)] = value
        stores.append(pltpu.make_async_copy(result.at[n], target, out_sem.at[n]))
        stores[-1].start()
        for a in (2 * n, 2 * n + 1):
            passes[a].wait()
            stores.append(pltpu.make_async_copy(passed.at[a], weight_grad.at[a], pass_sem.at[a]))
            stores[-1].start()
    for store in stores:
        store.wait()


def body(field, weights, cotangent):
    high, low = split_table(basis_table())
    table_in = np.concatenate([high, low], axis=0)
    table_out = np.concatenate([high.T, low.T, high.T], axis=1)
    table_in_y = table_in.reshape(256, GY, 2, 8).transpose(0, 2, 1, 3).reshape(256, N)
    table_out_y = table_out.reshape(GY, 2, 8, 384).transpose(1, 0, 2, 3).reshape(N, 384)
    tables = [jnp.asarray(t) for t in (table_in, table_out, table_in_y, table_out_y)]
    shape = jax.ShapeDtypeStruct
    anywhere = pl.BlockSpec(memory_space=pl.ANY)
    vmem = pltpu.VMEM
    dma = pltpu.SemaphoreType.DMA
    cell_block = vmem((2, 2, GX, 64, 256), F32)
    column_block = vmem((2, 2, GY, 8, 128), F32)
    received, grad = pl.pallas_call(
        kernel,
        out_shape=(shape((2, 2, GX, 64, 256), F32), shape((4, 4, 4, 8, 1024), F32)),
        in_specs=[anywhere] * 7,
        out_specs=(anywhere,) * 2,
        scratch_shapes=[
            vmem((2, 64, 16, 256), F32),
            vmem((4, 4, 4, 8, 1024), F32),
            vmem((256, N), BF16),
            vmem((N, 384), BF16),
            vmem((256, N), BF16),
            vmem((N, 384), BF16),
            vmem((128, 4096), BF16),
            vmem((128, 4096), F32),
            vmem((4, 4, 4, 8, 1024), F32),
            cell_block, cell_block,
            column_block, column_block,
            vmem((2, GY, 4, 128), F32), vmem((2, GX, 4, 4, 128), F32),
            vmem((2, GX, 4, 4, 128), F32), vmem((2, GY, 4, 128), F32),
            column_block, column_block,
            cell_block,
            dma((7,)), dma((1,)),
            dma((2, 2)), dma((2, 2)),
            dma((2, 2)), dma((2, 2)),
            dma((2,)), dma((2,)),
            dma((2,)), dma((2,)),
            dma((2, 2)), dma((2, 2)),
            dma((2, 2)), dma((2, 2)),
        ],
        compiler_params=pltpu.CompilerParams(
            collective_id=0, has_side_effects=True, vmem_limit_bytes=56 * 1024 * 1024
        ),
        name="spectral",
    )(field, cotangent, weights.reshape(4, 4, 4, 8, 1024), *tables)
    out = pl.pallas_call(
        finish_kernel,
        out_shape=(
            shape(field.shape, F32),
            shape(field.shape, F32),
            shape((4, 4, 4, 8, 1024), F32),
        ),
        in_specs=[anywhere] * 2,
        out_specs=(anywhere,) * 3,
        scratch_shapes=[
            cell_block,
            vmem((2, 64, 16, 256), F32),
            vmem((4, 4, 4, 8, 1024), F32),
            dma((2, 2)), dma((2,)), dma((4,)), dma((4,)),
        ],
        compiler_params=pltpu.CompilerParams(vmem_limit_bytes=56 * 1024 * 1024),
        name="finish",
    )(received, grad)
    return out[0], out[1], out[2].reshape(weights.shape)


def solution(mesh):
    in_specs = (P("gx", "gy", None), P("gy", "gx", None, None), P("gx", "gy", None))
    out_specs = (P("gx", "gy", None), P("gx", "gy", None), P("gy", "gx", None, None))
    return jax.shard_map(body, mesh=mesh, in_specs=in_specs, out_specs=out_specs, check_vma=False)
```

```python
import math

import jax
import jax.numpy as jnp
import numpy as np
from jax import lax
from jax.experimental import pallas as pl
from jax.experimental.pallas import tpu as pltpu
from jax.sharding import PartitionSpec as P

N = 512
MODES = 64
GX = 8
GY = 32
F32 = jnp.float32
BF16 = jnp.bfloat16
MESH = pl.DeviceIdType.MESH


def basis_table():
    k = np.arange(2 * MODES)[:, None]
    p = np.arange(N)[None, :]
    frequency = np.where(k < MODES, k, k - MODES + 1)
    angles = 2.0 * math.pi / N * ((frequency * p) % N)
    values = math.sqrt(2.0 / N) * np.where(k < MODES, np.cos(angles), np.sin(angles))
    return values.reshape(32, 4, N).transpose(1, 0, 2).reshape(128, N)


def split_table(values):
    values = values.astype(np.float32)
    high = values.astype(BF16)
    low = (values - high.astype(np.float32)).astype(BF16)
    return high, low


def halves(value):
    high = value.astype(BF16)
    return high, (value - high.astype(F32)).astype(BF16)


def spread_matrix():
    column = lax.broadcasted_iota(jnp.int32, (128, 4096), 1)
    row = lax.broadcasted_iota(jnp.int32, (128, 4096), 0)
    return jnp.where(column // 32 == row, 1.0, 0.0).astype(BF16)


def dot(a, b):
    return jnp.dot(a, b, preferred_element_type=F32)


def swap_blocks(v):
    lane = lax.broadcasted_iota(jnp.int32, v[0].shape, 1)
    low = lane < 64
    even = (lane // 32) % 2 == 0
    a0 = jnp.where(low, v[0], pltpu.roll(v[2], 64, 1))
    a1 = jnp.where(low, v[1], pltpu.roll(v[3], 64, 1))
    a2 = jnp.where(low, pltpu.roll(v[0], 64, 1), v[2])
    a3 = jnp.where(low, pltpu.roll(v[1], 64, 1), v[3])
    return [
        jnp.where(even, a0, pltpu.roll(a1, 32, 1)),
        jnp.where(even, pltpu.roll(a0, 96, 1), a1),
        jnp.where(even, a2, pltpu.roll(a3, 32, 1)),
        jnp.where(even, pltpu.roll(a2, 96, 1), a3),
    ]


def kernel(
    field, cotangent, weights, table_in, table_out, table_in_y, table_out_y,
    rf, weight_grad,
    cells, w, fwd, inv, fwd_y, inv_y, spread, expanded, wgrad,
    sa, ra, sb, rb, sc, rc, sd, rd, se, re, sf,
    in_sem, out_sem, a_send, a_recv, b_send, b_recv, c_send, c_recv,
    d_send, d_recv, e_send, e_recv, f_send, f_recv,
):
    i = lax.axis_index("gx")
    j = lax.axis_index("gy")

    def at(gx, gy):
        return {"gx": gx, "gy": gy}

    loads = [
        pltpu.make_async_copy(src, dst, in_sem.at[n])
        for n, (src, dst) in enumerate(
            [(field, cells.at[0]), (cotangent, cells.at[1]), (table_in, fwd), (table_in_y, fwd_y), (weights, w), (table_out_y, inv_y), (table_out, inv)]
        )
    ]
    for load in loads:
        load.start()

    barrier = pltpu.get_barrier_semaphore()

    def greet(gx, gy):
        pl.semaphore_signal(barrier, inc=1, device_id=at(gx, gy), device_id_type=MESH)

    def greet_x(v, carry):
        greet((i + v) % GX, j)
        return carry

    def greet_y(v, carry):
        other = (j + v) % GY
        greet(i, other)
        greet(j // 4, other)
        greet((i + v // 4) % GX, 4 * i + v % 4)
        return carry

    lax.fori_loop(0, GX, greet_x, 0)
    lax.fori_loop(0, GY, greet_y, 0)

    def send(src, dst, send_sem, recv_sem, gx, gy):
        here = jnp.logical_and(gx == i, gy == j)

        @pl.when(jnp.logical_not(here))
        def _():
            pltpu.make_async_remote_copy(
                src_ref=src, dst_ref=dst, send_sem=send_sem, recv_sem=recv_sem,
                device_id=at(gx, gy), device_id_type=MESH,
            ).start()

        @pl.when(here)
        def _():
            pltpu.make_async_copy(src, dst, recv_sem).start()

    def wait(ref, sem):
        pltpu.make_async_copy(ref, ref, sem).wait()

    def pack_cells(n, u):
        for h in range(2):
            v = [cells[n, :, 4 * u + s, pl.ds(128 * h, 128)] for s in range(4)]
            for b, value in enumerate(swap_blocks(v)):
                sa[n, u, 4 * h + b] = value

    def send_x(src, dst, send_sem, recv_sem, n, u):
        for v in range(1, GX):
            other = (i + v) % GX
            pltpu.make_async_remote_copy(
                src_ref=src.at[n, u, other], dst_ref=dst.at[n, u, i],
                send_sem=send_sem.at[n, u], recv_sem=recv_sem.at[n, u],
                device_id=at(other, j), device_id_type=MESH,
            ).start()
        pltpu.make_async_copy(src.at[n, u, i], dst.at[n, u, i], recv_sem.at[n, u]).start()

    def send_cells(n, u):
        send_x(sa, ra, a_send, a_recv, n, u)

    def send_result(n, u):
        send_x(sf, rf, f_send, f_recv, n, u)

    def project(table, data):
        high, low = halves(data)
        first = dot(table, high)
        return first[:128] + first[128:] + dot(table[:128], low)

    def expand(table, data):
        high, low = halves(data)
        return dot(table, jnp.concatenate([high, high, low], axis=0))

    def project_x(n, u):
        wait(ra.at[n, u], a_recv.at[n, u])
        modes = project(fwd[...], ra[n, u].reshape(N, 128))
        v = [modes[32 * r : 32 * r + 32] for r in range(4)]
        for s, value in enumerate(swap_blocks(v)):
            sb[n, u, :, s, :] = value
        send_columns(n, u, sb, rb, b_send, b_recv)

    def send_columns(n, u, src, dst, send_sem, recv_sem):
        def step(v, carry):
            other = (j + v) % GY
            send(src.at[n, u, other], dst.at[n, u, j], send_sem.at[n, u], recv_sem.at[n, u], i, other)
            return carry

        lax.fori_loop(0, GY, step, 0)

    def project_y(n):
        parts = []
        for half in range(2):
            rows = []
            for u in (2 * half, 2 * half + 1):
                wait(rb.at[n, u], b_recv.at[n, u])
                rows += [rb[n, u, :, s, :] for s in range(4)]
            table = fwd_y[:, pl.ds(256 * half, 256)]
            parts.append(project(table, jnp.concatenate(rows, axis=0)))
        modes = parts[0] + parts[1]
        for a in range(4):
            sc[n, :, a, :] = modes[32 * a : 32 * a + 32]

        def step(v, carry):
            other = (j + v) % GY
            send(sc.at[n, other], rc.at[n, i, j % 4], c_send.at[n], c_recv.at[n], j // 4, other)
            return carry

        lax.fori_loop(0, GY, step, 0)

    def owned_modes(n):
        wait(rc.at[n], c_recv.at[n])
        return jnp.concatenate([rc[n, :, q, a, :] for a in range(4) for q in range(4)], axis=0)

    def send_mixed(n, value):
        for a in range(4):
            for q in range(4):
                row = 8 * (4 * a + q)
                sd[n, :, q, a, :] = value[row : row + 8]

        def step(v, carry):
            z = (i + v // 4) % GX
            q = v % 4
            send(sd.at[n, z, q], rd.at[n, j], d_send.at[n], d_recv.at[n], z, 4 * i + q)
            return carry

        lax.fori_loop(0, GY, step, 0)

    def mix():
        high, low = halves(owned_modes(0))
        folded = []
        for r in range(4):
            part = spread[:, pl.ds(1024 * r, 1024)]
            wide = dot(high, part) + dot(low, part)
            expanded[:, pl.ds(1024 * r, 1024)] = wide
            product = wide * w[:, :, r].reshape(128, 1024)
            total = product[:, :128]
            for t in range(1, 8):
                total = total + product[:, 128 * t : 128 * t + 128]
            folded.append(total)
        parts = swap_blocks(folded)
        send_mixed(0, (parts[0] + parts[1]) + (parts[2] + parts[3]))

    def mix_back():
        grads = owned_modes(1)
        tiled = swap_blocks([grads] * 4)
        total = None
        for r in range(4):
            part = spread[:, pl.ds(1024 * r, 1024)]
            product = w[:, :, r].reshape(128, 1024) * jnp.concatenate([tiled[r]] * 8, axis=1)
            high, low = halves(product)
            dims = (((1,), (1,)), ((), ()))
            term = lax.dot_general(high, part, dims, preferred_element_type=F32)
            term = term + lax.dot_general(low, part, dims, preferred_element_type=F32)
            total = term if total is None else total + term
        send_mixed(1, total)
        return tiled

    def outer(tiled):
        for r in range(4):
            value = expanded[:, pl.ds(1024 * r, 1024)] * jnp.concatenate([tiled[r]] * 8, axis=1)
            wgrad[:, :, r] = value.reshape(4, 4, 8, 1024)


    def expand_y(n):
        wait(rd.at[n], d_recv.at[n])
        modes = jnp.concatenate([rd[n, :, a, :] for a in range(4)], axis=0)
        for u in range(4):
            rows = expand(inv_y[pl.ds(128 * u, 128), :], modes)
            for s in range(4):
                se[n, u, :, s, :] = rows[32 * s : 32 * s + 32]
            send_columns(n, u, se, re, e_send, e_recv)

    def expand_x(n, u):
        wait(re.at[n, u], e_recv.at[n, u])
        v = [re[n, u, :, s, :] for s in range(4)]
        modes = jnp.concatenate(swap_blocks(v), axis=0)
        sf[n, u] = expand(inv[...], modes).reshape(GX, 64, 128)

    loads[0].wait()
    for u in range(4):
        pack_cells(0, u)
    pl.semaphore_wait(barrier, GX + 3 * GY)
    for u in range(4):
        send_cells(0, u)
    loads[1].wait()
    for u in range(4):
        pack_cells(1, u)
    spread[...] = spread_matrix()
    for load in loads[2:]:
        load.wait()

    project_x(0, 0)
    project_x(0, 1)
    send_cells(1, 0)
    send_cells(1, 1)
    project_x(0, 2)
    project_x(0, 3)
    send_cells(1, 2)
    send_cells(1, 3)
    project_y(0)
    for u in range(4):
        project_x(1, u)
    mix()
    project_y(1)
    expand_y(0)
    tiled = mix_back()
    for u in range(2):
        expand_x(0, u)
        send_result(0, u)
    for u in range(2, 4):
        expand_x(0, u)
    expand_y(1)
    for u in range(2, 4):
        send_result(0, u)
    outer(tiled)
    store = pltpu.make_async_copy(wgrad, weight_grad, out_sem.at[0])
    store.start()
    for u in range(4):
        expand_x(1, u)
        send_result(1, u)

    for n in range(2):
        for u in range(4):
            wait(rf.at[n, u], f_recv.at[n, u])
            wait(sa.at[n, u, pl.ds(0, GX - 1)], a_send.at[n, u])
            wait(sb.at[n, u, pl.ds(0, GY - 1)], b_send.at[n, u])
            wait(se.at[n, u, pl.ds(0, GY - 1)], e_send.at[n, u])
            wait(sf.at[n, u, pl.ds(0, GX - 1)], f_send.at[n, u])

    inside = i == j // 4

    @pl.when(inside)
    def _():
        for n in range(2):
            wait(sc.at[n, pl.ds(0, GY - 1)], c_send.at[n])
            wait(rd.at[n, pl.ds(0, GY - 1)], d_send.at[n])

    @pl.when(jnp.logical_not(inside))
    def _():
        for n in range(2):
            wait(sc.at[n], c_send.at[n])
            wait(rd.at[n], d_send.at[n])

    store.wait()


def finish_kernel(
    received, grad, output_field, field_grad, weight_grad,
    cells, result, passed, load_sem, out_sem, grad_sem, pass_sem,
):
    loads = [
        pltpu.make_async_copy(received.at[n, u], cells.at[n, u], load_sem.at[n, u])
        for n in range(2)
        for u in range(4)
    ]
    passes = [pltpu.make_async_copy(grad.at[a], passed.at[a], grad_sem.at[a]) for a in range(4)]
    for load in loads[:4] + passes + loads[4:]:
        load.start()
    stores = []
    for n, target in enumerate([output_field, field_grad]):
        for u in range(4):
            loads[4 * n + u].wait()
            for h in range(2):
                v = [cells[n, u, 4 * h + b] for b in range(4)]
                for s, value in enumerate(swap_blocks(v)):
                    result[n, :, 4 * u + s, pl.ds(128 * h, 128)] = value
            if u % 2 == 1:
                rows = pl.ds(4 * u - 4, 8)
                stores.append(
                    pltpu.make_async_copy(result.at[n, :, rows], target.at[:, rows], out_sem.at[n, u // 2])
                )
                stores[-1].start()
                a = 2 * n + u // 2
                passes[a].wait()
                stores.append(pltpu.make_async_copy(passed.at[a], weight_grad.at[a], pass_sem.at[a]))
                stores[-1].start()
    for store in stores:
        store.wait()


def body(field, weights, cotangent):
    high, low = split_table(basis_table())
    table_in = np.concatenate([high, low], axis=0)
    table_out = np.concatenate([high.T, low.T, high.T], axis=1)
    table_in_y = table_in.reshape(256, GY, 4, 4).transpose(0, 2, 3, 1).reshape(256, N)
    table_out_y = table_out.reshape(GY, 4, 4, 384).transpose(1, 2, 0, 3).reshape(N, 384)
    tables = [jnp.asarray(t) for t in (table_in, table_out, table_in_y, table_out_y)]
    shape = jax.ShapeDtypeStruct
    anywhere = pl.BlockSpec(memory_space=pl.ANY)
    vmem = pltpu.VMEM
    dma = pltpu.SemaphoreType.DMA
    cell_block = vmem((2, 4, GX, 64, 128), F32)
    column_block = vmem((2, 4, GY, 4, 128), F32)
    received, grad = pl.pallas_call(
        kernel,
        out_shape=(shape((2, 4, GX, 64, 128), F32), shape((4, 4, 4, 8, 1024), F32)),
        in_specs=[anywhere] * 7,
        out_specs=(anywhere,) * 2,
        scratch_shapes=[
            vmem((2, 64, 16, 256), F32),
            vmem((4, 4, 4, 8, 1024), F32),
            vmem((256, N), BF16),
            vmem((N, 384), BF16),
            vmem((256, N), BF16),
            vmem((N, 384), BF16),
            vmem((128, 4096), BF16),
            vmem((128, 4096), F32),
            vmem((4, 4, 4, 8, 1024), F32),
            cell_block, cell_block,
            column_block, column_block,
            vmem((2, GY, 4, 128), F32), vmem((2, GX, 4, 4, 128), F32),
            vmem((2, GX, 4, 4, 128), F32), vmem((2, GY, 4, 128), F32),
            column_block, column_block,
            cell_block,
            dma((7,)), dma((1,)),
            dma((2, 4)), dma((2, 4)),
            dma((2, 4)), dma((2, 4)),
            dma((2,)), dma((2,)),
            dma((2,)), dma((2,)),
            dma((2, 4)), dma((2, 4)),
            dma((2, 4)), dma((2, 4)),
        ],
        compiler_params=pltpu.CompilerParams(
            collective_id=0, has_side_effects=True, vmem_limit_bytes=56 * 1024 * 1024
        ),
        name="spectral",
    )(field, cotangent, weights.reshape(4, 4, 4, 8, 1024), *tables)
    out = pl.pallas_call(
        finish_kernel,
        out_shape=(
            shape(field.shape, F32),
            shape(field.shape, F32),
            shape((4, 4, 4, 8, 1024), F32),
        ),
        in_specs=[anywhere] * 2,
        out_specs=(anywhere,) * 3,
        scratch_shapes=[
            cell_block,
            vmem((2, 64, 16, 256), F32),
            vmem((4, 4, 4, 8, 1024), F32),
            dma((2, 4)), dma((2, 2)), dma((4,)), dma((4,)),
        ],
        compiler_params=pltpu.CompilerParams(vmem_limit_bytes=56 * 1024 * 1024),
        name="finish",
    )(received, grad)
    return out[0], out[1], out[2].reshape(weights.shape)


def solution(mesh):
    in_specs = (P("gx", "gy", None), P("gy", "gx", None, None), P("gx", "gy", None))
    out_specs = (P("gx", "gy", None), P("gx", "gy", None), P("gy", "gx", None, None))
    return jax.shard_map(body, mesh=mesh, in_specs=in_specs, out_specs=out_specs, check_vma=False)
```

```python
import math

import jax
import jax.numpy as jnp
import numpy as np
from jax import lax
from jax.experimental import pallas as pl
from jax.experimental.pallas import tpu as pltpu
from jax.sharding import PartitionSpec as P

N = 512
MODES = 64
GX = 8
GY = 32
PEERS = ((1, 0), (0, 1), (3, 0), (2, 1), (1, 1), (2, 0), (3, 1))
F32 = jnp.float32
BF16 = jnp.bfloat16
MESH = pl.DeviceIdType.MESH


def basis_table():
    k = np.arange(2 * MODES)[:, None]
    p = np.arange(N)[None, :]
    frequency = np.where(k < MODES, k, k - MODES + 1)
    angles = 2.0 * math.pi / N * ((frequency * p) % N)
    values = math.sqrt(2.0 / N) * np.where(k < MODES, np.cos(angles), np.sin(angles))
    return values.reshape(32, 4, N).transpose(1, 0, 2).reshape(128, N)


def split_table(values):
    values = values.astype(np.float32)
    high = values.astype(BF16)
    low = (values - high.astype(np.float32)).astype(BF16)
    return high, low


def halves(value):
    high = value.astype(BF16)
    return high, (value - high.astype(F32)).astype(BF16)


def spread_matrix():
    column = lax.broadcasted_iota(jnp.int32, (128, 4096), 1)
    row = lax.broadcasted_iota(jnp.int32, (128, 4096), 0)
    return jnp.where(column // 32 == row, 1.0, 0.0).astype(BF16)


def dot(a, b):
    return jnp.dot(a, b, preferred_element_type=F32)


def swap_blocks(v):
    lane = lax.broadcasted_iota(jnp.int32, v[0].shape, 1)
    low = lane < 64
    even = (lane // 32) % 2 == 0
    a0 = jnp.where(low, v[0], pltpu.roll(v[2], 64, 1))
    a1 = jnp.where(low, v[1], pltpu.roll(v[3], 64, 1))
    a2 = jnp.where(low, pltpu.roll(v[0], 64, 1), v[2])
    a3 = jnp.where(low, pltpu.roll(v[1], 64, 1), v[3])
    return [
        jnp.where(even, a0, pltpu.roll(a1, 32, 1)),
        jnp.where(even, pltpu.roll(a0, 96, 1), a1),
        jnp.where(even, a2, pltpu.roll(a3, 32, 1)),
        jnp.where(even, pltpu.roll(a2, 96, 1), a3),
    ]


def kernel(
    field, cotangent, weights, table_in, table_out, table_in_y, table_out_y,
    rf, weight_grad,
    cells, w, fwd, inv, fwd_y, inv_y, spread, expanded, wgrad,
    sa, ra, sb, rb, sc, rc, sd, rd, se, re, sf,
    in_sem, out_sem, a_send, a_recv, b_send, b_recv, c_send, c_recv,
    d_send, d_recv, e_send, e_recv, f_send, f_recv,
):
    i = lax.axis_index("gx")
    j = lax.axis_index("gy")

    def at(gx, gy):
        return {"gx": gx, "gy": gy}

    loads = [
        pltpu.make_async_copy(src, dst, in_sem.at[n])
        for n, (src, dst) in enumerate(
            [(field, cells.at[0]), (cotangent, cells.at[1]), (table_in, fwd), (table_in_y, fwd_y), (weights, w), (table_out_y, inv_y), (table_out, inv)]
        )
    ]
    for load in loads:
        load.start()

    barrier = pltpu.get_barrier_semaphore()

    def greet(gx, gy):
        pl.semaphore_signal(barrier, inc=1, device_id=at(gx, gy), device_id_type=MESH)

    def greet_x(v, carry):
        greet((i + v) % GX, j)
        return carry

    def greet_y(v, carry):
        other = (j + v) % GY
        greet(i, other)
        greet(j // 4, other)
        greet((i + v // 4) % GX, 4 * i + v % 4)
        return carry

    lax.fori_loop(0, GX, greet_x, 0)
    lax.fori_loop(0, GY, greet_y, 0)

    def send(src, dst, send_sem, recv_sem, gx, gy):
        here = jnp.logical_and(gx == i, gy == j)

        @pl.when(jnp.logical_not(here))
        def _():
            pltpu.make_async_remote_copy(
                src_ref=src, dst_ref=dst, send_sem=send_sem, recv_sem=recv_sem,
                device_id=at(gx, gy), device_id_type=MESH,
            ).start()

        @pl.when(here)
        def _():
            pltpu.make_async_copy(src, dst, recv_sem).start()

    def wait(ref, sem):
        pltpu.make_async_copy(ref, ref, sem).wait()

    def pack_cells(n, u):
        for h in range(2):
            v = [cells[n, :, 4 * u + s, pl.ds(128 * h, 128)] for s in range(4)]
            for b, value in enumerate(swap_blocks(v)):
                sa[n, u, 4 * h + b] = value

    def send_x(src, dst, send_sem, recv_sem, n, u):
        for dy, dx in PEERS:
            dy = jnp.where(j % 2 == 0, dy, 4 - dy)
            other = (i // 2 + dy) % 4 * 2 + (i + dx) % 2
            pltpu.make_async_remote_copy(
                src_ref=src.at[n, u, other], dst_ref=dst.at[n, u, i],
                send_sem=send_sem.at[n, u], recv_sem=recv_sem.at[n, u],
                device_id=at(other, j), device_id_type=MESH,
            ).start()
        pltpu.make_async_copy(src.at[n, u, i], dst.at[n, u, i], recv_sem.at[n, u]).start()

    def send_cells(n, u):
        send_x(sa, ra, a_send, a_recv, n, u)

    def send_result(n, u):
        send_x(sf, rf, f_send, f_recv, n, u)

    def project(table, data):
        high, low = halves(data)
        first = dot(table, high)
        return first[:128] + first[128:] + dot(table[:128], low)

    def expand(table, data):
        high, low = halves(data)
        return dot(table, jnp.concatenate([high, high, low], axis=0))

    def project_x(n, u):
        wait(ra.at[n, u], a_recv.at[n, u])
        modes = project(fwd[...], ra[n, u].reshape(N, 128))
        v = [modes[32 * r : 32 * r + 32] for r in range(4)]
        for s, value in enumerate(swap_blocks(v)):
            sb[n, u, :, s, :] = value
        send_columns(n, u, sb, rb, b_send, b_recv)

    def send_columns(n, u, src, dst, send_sem, recv_sem):
        def step(v, carry):
            other = (j + v) % GY
            send(src.at[n, u, other], dst.at[n, u, j], send_sem.at[n, u], recv_sem.at[n, u], i, other)
            return carry

        lax.fori_loop(0, GY, step, 0)

    def project_y(n):
        parts = []
        for half in range(2):
            rows = []
            for u in (2 * half, 2 * half + 1):
                wait(rb.at[n, u], b_recv.at[n, u])
                rows += [rb[n, u, :, s, :] for s in range(4)]
            table = fwd_y[:, pl.ds(256 * half, 256)]
            parts.append(project(table, jnp.concatenate(rows, axis=0)))
        modes = parts[0] + parts[1]
        for a in range(4):
            sc[n, :, a, :] = modes[32 * a : 32 * a + 32]

        def step(v, carry):
            other = (j + v) % GY
            send(sc.at[n, other], rc.at[n, i, j % 4], c_send.at[n], c_recv.at[n], j // 4, other)
            return carry

        lax.fori_loop(0, GY, step, 0)

    def owned_modes(n):
        wait(rc.at[n], c_recv.at[n])
        return jnp.concatenate([rc[n, :, q, a, :] for a in range(4) for q in range(4)], axis=0)

    def send_mixed(n, value):
        for a in range(4):
            for q in range(4):
                row = 8 * (4 * a + q)
                sd[n, :, q, a, :] = value[row : row + 8]

        def step(v, carry):
            z = (i + v // 4) % GX
            q = v % 4
            send(sd.at[n, z, q], rd.at[n, j], d_send.at[n], d_recv.at[n], z, 4 * i + q)
            return carry

        lax.fori_loop(0, GY, step, 0)

    def mix():
        high, low = halves(owned_modes(0))
        folded = []
        for r in range(4):
            part = spread[:, pl.ds(1024 * r, 1024)]
            wide = dot(high, part) + dot(low, part)
            expanded[:, pl.ds(1024 * r, 1024)] = wide
            product = wide * w[:, :, r].reshape(128, 1024)
            total = product[:, :128]
            for t in range(1, 8):
                total = total + product[:, 128 * t : 128 * t + 128]
            folded.append(total)
        parts = swap_blocks(folded)
        send_mixed(0, (parts[0] + parts[1]) + (parts[2] + parts[3]))

    def mix_back():
        grads = owned_modes(1)
        tiled = swap_blocks([grads] * 4)
        total = None
        for r in range(4):
            part = spread[:, pl.ds(1024 * r, 1024)]
            product = w[:, :, r].reshape(128, 1024) * jnp.concatenate([tiled[r]] * 8, axis=1)
            high, low = halves(product)
            dims = (((1,), (1,)), ((), ()))
            term = lax.dot_general(high, part, dims, preferred_element_type=F32)
            term = term + lax.dot_general(low, part, dims, preferred_element_type=F32)
            total = term if total is None else total + term
        send_mixed(1, total)
        return tiled

    def outer(tiled):
        for r in range(4):
            value = expanded[:, pl.ds(1024 * r, 1024)] * jnp.concatenate([tiled[r]] * 8, axis=1)
            wgrad[:, :, r] = value.reshape(4, 4, 8, 1024)


    def expand_y(n):
        wait(rd.at[n], d_recv.at[n])
        modes = jnp.concatenate([rd[n, :, a, :] for a in range(4)], axis=0)
        for u in range(4):
            rows = expand(inv_y[pl.ds(128 * u, 128), :], modes)
            for s in range(4):
                se[n, u, :, s, :] = rows[32 * s : 32 * s + 32]
            send_columns(n, u, se, re, e_send, e_recv)

    def expand_x(n, u):
        wait(re.at[n, u], e_recv.at[n, u])
        v = [re[n, u, :, s, :] for s in range(4)]
        modes = jnp.concatenate(swap_blocks(v), axis=0)
        sf[n, u] = expand(inv[...], modes).reshape(GX, 64, 128)

    loads[0].wait()
    for u in range(4):
        pack_cells(0, u)
    pl.semaphore_wait(barrier, GX + 3 * GY)
    for u in range(4):
        send_cells(0, u)
    loads[1].wait()
    for u in range(4):
        pack_cells(1, u)
    spread[...] = spread_matrix()
    for load in loads[2:]:
        load.wait()

    project_x(0, 0)
    project_x(0, 1)
    send_cells(1, 0)
    send_cells(1, 1)
    project_x(0, 2)
    project_x(0, 3)
    send_cells(1, 2)
    send_cells(1, 3)
    project_y(0)
    for u in range(4):
        project_x(1, u)
    mix()
    project_y(1)
    expand_y(0)
    tiled = mix_back()
    for u in range(2):
        expand_x(0, u)
        send_result(0, u)
    for u in range(2, 4):
        expand_x(0, u)
    expand_y(1)
    for u in range(2, 4):
        send_result(0, u)
    outer(tiled)
    store = pltpu.make_async_copy(wgrad, weight_grad, out_sem.at[0])
    store.start()
    for u in range(4):
        expand_x(1, u)
        send_result(1, u)

    for n in range(2):
        for u in range(4):
            wait(rf.at[n, u], f_recv.at[n, u])
            wait(sa.at[n, u, pl.ds(0, GX - 1)], a_send.at[n, u])
            wait(sb.at[n, u, pl.ds(0, GY - 1)], b_send.at[n, u])
            wait(se.at[n, u, pl.ds(0, GY - 1)], e_send.at[n, u])
            wait(sf.at[n, u, pl.ds(0, GX - 1)], f_send.at[n, u])

    inside = i == j // 4

    @pl.when(inside)
    def _():
        for n in range(2):
            wait(sc.at[n, pl.ds(0, GY - 1)], c_send.at[n])
            wait(rd.at[n, pl.ds(0, GY - 1)], d_send.at[n])

    @pl.when(jnp.logical_not(inside))
    def _():
        for n in range(2):
            wait(sc.at[n], c_send.at[n])
            wait(rd.at[n], d_send.at[n])

    store.wait()


def finish_kernel(
    received, grad, output_field, field_grad, weight_grad,
    cells, result, passed, load_sem, out_sem, grad_sem, pass_sem,
):
    loads = [
        pltpu.make_async_copy(received.at[n, u], cells.at[n, u], load_sem.at[n, u])
        for n in range(2)
        for u in range(4)
    ]
    passes = [pltpu.make_async_copy(grad.at[a], passed.at[a], grad_sem.at[a]) for a in range(4)]
    for load in loads[:4] + passes + loads[4:]:
        load.start()
    stores = []
    for n, target in enumerate([output_field, field_grad]):
        for u in range(4):
            loads[4 * n + u].wait()
            for h in range(2):
                v = [cells[n, u, 4 * h + b] for b in range(4)]
                for s, value in enumerate(swap_blocks(v)):
                    result[n, :, 4 * u + s, pl.ds(128 * h, 128)] = value
            if u % 2 == 1:
                rows = pl.ds(4 * u - 4, 8)
                stores.append(
                    pltpu.make_async_copy(result.at[n, :, rows], target.at[:, rows], out_sem.at[n, u // 2])
                )
                stores[-1].start()
                a = 2 * n + u // 2
                passes[a].wait()
                stores.append(pltpu.make_async_copy(passed.at[a], weight_grad.at[a], pass_sem.at[a]))
                stores[-1].start()
    for store in stores:
        store.wait()


def body(field, weights, cotangent):
    high, low = split_table(basis_table())
    table_in = np.concatenate([high, low], axis=0)
    table_out = np.concatenate([high.T, low.T, high.T], axis=1)
    table_in_y = table_in.reshape(256, GY, 4, 4).transpose(0, 2, 3, 1).reshape(256, N)
    table_out_y = table_out.reshape(GY, 4, 4, 384).transpose(1, 2, 0, 3).reshape(N, 384)
    tables = [jnp.asarray(t) for t in (table_in, table_out, table_in_y, table_out_y)]
    shape = jax.ShapeDtypeStruct
    anywhere = pl.BlockSpec(memory_space=pl.ANY)
    vmem = pltpu.VMEM
    dma = pltpu.SemaphoreType.DMA
    cell_block = vmem((2, 4, GX, 64, 128), F32)
    column_block = vmem((2, 4, GY, 4, 128), F32)
    received, grad = pl.pallas_call(
        kernel,
        out_shape=(shape((2, 4, GX, 64, 128), F32), shape((4, 4, 4, 8, 1024), F32)),
        in_specs=[anywhere] * 7,
        out_specs=(anywhere,) * 2,
        scratch_shapes=[
            vmem((2, 64, 16, 256), F32),
            vmem((4, 4, 4, 8, 1024), F32),
            vmem((256, N), BF16),
            vmem((N, 384), BF16),
            vmem((256, N), BF16),
            vmem((N, 384), BF16),
            vmem((128, 4096), BF16),
            vmem((128, 4096), F32),
            vmem((4, 4, 4, 8, 1024), F32),
            cell_block, cell_block,
            column_block, column_block,
            vmem((2, GY, 4, 128), F32), vmem((2, GX, 4, 4, 128), F32),
            vmem((2, GX, 4, 4, 128), F32), vmem((2, GY, 4, 128), F32),
            column_block, column_block,
            cell_block,
            dma((7,)), dma((1,)),
            dma((2, 4)), dma((2, 4)),
            dma((2, 4)), dma((2, 4)),
            dma((2,)), dma((2,)),
            dma((2,)), dma((2,)),
            dma((2, 4)), dma((2, 4)),
            dma((2, 4)), dma((2, 4)),
        ],
        compiler_params=pltpu.CompilerParams(
            collective_id=0, has_side_effects=True, vmem_limit_bytes=56 * 1024 * 1024
        ),
        name="spectral",
    )(field, cotangent, weights.reshape(4, 4, 4, 8, 1024), *tables)
    out = pl.pallas_call(
        finish_kernel,
        out_shape=(
            shape(field.shape, F32),
            shape(field.shape, F32),
            shape((4, 4, 4, 8, 1024), F32),
        ),
        in_specs=[anywhere] * 2,
        out_specs=(anywhere,) * 3,
        scratch_shapes=[
            cell_block,
            vmem((2, 64, 16, 256), F32),
            vmem((4, 4, 4, 8, 1024), F32),
            dma((2, 4)), dma((2, 2)), dma((4,)), dma((4,)),
        ],
        compiler_params=pltpu.CompilerParams(vmem_limit_bytes=56 * 1024 * 1024),
        name="finish",
    )(received, grad)
    return out[0], out[1], out[2].reshape(weights.shape)


def solution(mesh):
    in_specs = (P("gx", "gy", None), P("gy", "gx", None, None), P("gx", "gy", None))
    out_specs = (P("gx", "gy", None), P("gx", "gy", None), P("gy", "gx", None, None))
    return jax.shard_map(body, mesh=mesh, in_specs=in_specs, out_specs=out_specs, check_vma=False)
```
